256 devices in a mesh: row: 64 (over y, x, z_lo), col: 4 (over z_hi, core).
Axes of the slice: x: 4, y: 4, z: 8 (z_hi: 2, z_lo: 4; z = z_hi * 4 + z_lo), core: 2. Of those that a mesh axis runs over, the one named last changes fastest.
Arguments:
- row_feats: bfloat16 [262144, 128], P(('row', 'col')), may hold values from -1.2 to 1.2
- row_probes: bfloat16 [16, 262144], P(None, ('row', 'col')), may hold values from -6 to 6
- col_feats: bfloat16 [4, 128, 8192], P('col', None, 'row'), may hold values from -1.2 to 1.2
- col_probes: bfloat16 [4, 16, 8192], P('col', None, 'row'), may hold values from -6 to 6
- lengthscale: float32 [128], replicated, may hold values from 0.6 to 1.6
- outputscale: float32 [1], replicated, may hold values from 0.08 to 0.3
- tile_ids: int32 [64, 4, 4], P('row', 'col'), may hold values from 0 to 7, as said below
- tile_counts: int32 [64, 4], P('row', 'col'), may hold values from 1 to 4, as said below
Outputs:
- row_result: float32 [16, 262144], P(None, ('row', 'col'))
- col_result: float32 [4, 16, 8192], P('col', None, 'row')
The draws below stay inside these ranges and needn't reach their ends.
Inputs may be any that keep to these rules, and one draw needn't show every extreme that they name: `tile_ids`: within one device's list the 4 entries are distinct; entries at or past the count are ignored. `tile_counts`: devices of the first row index hold exactly 4 live tiles.
All inputs are finite; a program needn't handle non-finite values.
Results may differ from the reference program's by a relative error of at most 0.014.
Values may be sent and summed in bfloat16 or wider, within the bound.
A program may use at most 64 MiB of HBM per device.

```python
import math
import jax
import jax.numpy as jnp
from jax import lax

D = 128
P_SIZE = 16
BLK = 2048
RB = 2
CB = 4
TILES_DEV = 4
NR = 262144
NC = 8192
N_ROW = 64
N_COL = 4


def shared_terms(key):
    feature_gain = jax.random.uniform(jax.random.fold_in(key, 101), (D,), jnp.float32, 0.08, 0.2)
    return feature_gain


def assemble(latent, noise_part, feature_gain):
    repeat = feature_gain.shape[0] // latent.shape[-1]
    spread_latent = jnp.concatenate([latent] * repeat, axis=-1)
    return spread_latent * feature_gain + noise_part


def draw_row_feats(key, part):
    feature_gain = shared_terms(key)
    key = jax.random.fold_in(key, 7)
    latent_key, noise_key = jax.random.split(key, 2)
    latent = jnp.clip(jax.random.normal(latent_key, (NR, 16), jnp.float32), -4.0, 4.0)
    noise_part = 0.08 * jnp.clip(jax.random.normal(noise_key, (NR, D), jnp.float32), -4.0, 4.0)
    return assemble(latent, noise_part, feature_gain).astype(jnp.bfloat16)


def draw_col_feats(key, part):
    feature_gain = shared_terms(key)
    key = jax.random.fold_in(key, 13)
    latent_key, noise_key = jax.random.split(key, 2)
    latent = jnp.clip(jax.random.normal(latent_key, (N_COL, NC, 16), jnp.float32), -4.0, 4.0)
    noise_part = 0.08 * jnp.clip(jax.random.normal(noise_key, (N_COL, NC, D), jnp.float32), -4.0, 4.0)
    points = assemble(latent, noise_part, feature_gain)
    return jnp.swapaxes(points, 1, 2).astype(jnp.bfloat16)


def draw_tile_ids(key, part):
    key = jax.random.fold_in(key, 11)
    keys = jax.random.split(key, N_ROW * N_COL)
    chosen = jax.vmap(lambda one_key: jax.random.permutation(one_key, RB * CB)[:TILES_DEV])(keys)
    return chosen.reshape(N_ROW, N_COL, TILES_DEV).astype(jnp.int32)


def draw_tile_counts(key, part):
    key = jax.random.fold_in(key, 23)
    row_group = jnp.arange(N_ROW, dtype=jnp.int32)[:, None]
    baseline = 1 + (TILES_DEV - 1) * (N_ROW - 1 - row_group) // max(N_ROW - 1, 1)
    jitter = jax.random.randint(key, (N_ROW, N_COL), -1, 2, dtype=jnp.int32)
    jitter = jnp.where(row_group == 0, 0, jitter)
    return jnp.clip(baseline + jitter, 1, TILES_DEV).astype(jnp.int32)


def block_scale(own_key, dims, pieces, low, largest):
    loudness, own = 1.0, jax.random.fold_in(own_key, 6)
    for dim, parts in pieces:
        draws = jnp.exp(jax.random.uniform(jax.random.fold_in(own, dim), (parts,), jnp.float32, low / len(pieces), largest / len(pieces)))
        loudness = loudness * jnp.repeat(draws, dims[dim] // parts).reshape([-1 if axis == dim else 1 for axis in range(len(dims))])
    return loudness


def noise(rng, extent, width, most, shards=(), kind=jnp.bfloat16):
    level = block_scale(rng, extent, shards, -0.22, 0.18) if shards else 1.0
    entries = jax.random.normal(rng, extent, jnp.float32) * width * level
    return jnp.minimum(jnp.maximum(entries, -most), most).astype(kind)


def setup_inputs(seed: int = 0) -> dict:
    splits = jax.random.split(jax.random.key(seed), 9)
    row_feats = draw_row_feats(jax.random.fold_in(splits[8], 71), 0)
    row_probes = noise(splits[1], (P_SIZE, NR), 1.0, 6.0, ((1, 256),))
    col_feats = draw_col_feats(jax.random.fold_in(splits[8], 71), 0)
    col_probes = noise(splits[3], (N_COL, P_SIZE, NC), 1.0, 6.0, ((0, 4), (2, 64)))
    lengthscale = jnp.clip(jnp.exp(jax.random.uniform(splits[4], (D,), jnp.float32, math.log(0.6), math.log(1.6))), 0.6, 1.6)
    outputscale = jnp.clip(jax.random.uniform(splits[5], (1,), jnp.float32, 0.08, 0.3), 0.08, 0.3)
    tile_ids = draw_tile_ids(jax.random.fold_in(splits[8], 71), 0)
    tile_counts = draw_tile_counts(jax.random.fold_in(splits[8], 71), 0)
    return dict(row_feats=row_feats, row_probes=row_probes, col_feats=col_feats, col_probes=col_probes, lengthscale=lengthscale, outputscale=outputscale, tile_ids=tile_ids, tile_counts=tile_counts)


def kernel_block(row_part, row_norm, col_part, col_norm, factor):
    product = jnp.dot(row_part, col_part, preferred_element_type=jnp.float32)
    distance = row_norm[:, None] + col_norm[None, :] - 2.0 * product
    return (factor * jnp.exp(-0.5 * distance)).astype(jnp.bfloat16)


def reference(row_feats, row_probes, col_feats, col_probes, lengthscale, outputscale, tile_ids, tile_counts):
    row_z = (row_feats.astype(jnp.float32) / lengthscale[None, :]).astype(jnp.bfloat16)
    col_z = (col_feats.astype(jnp.float32) / lengthscale[None, :, None]).astype(jnp.bfloat16)
    row_sq = jnp.sum(jnp.square(row_z.astype(jnp.float32)), axis=1)
    col_sq = jnp.sum(jnp.square(col_z.astype(jnp.float32)), axis=1)
    factor = outputscale[0]
    row_total = jnp.zeros((P_SIZE, NR), jnp.float32)
    col_total = jnp.zeros((N_COL, P_SIZE, NC), jnp.float32)

    def visit_slot(slot_index, totals):
        slot_index = jnp.asarray(slot_index).astype(jnp.int32)
        row_group = slot_index // (N_COL * TILES_DEV)
        col_group = (slot_index // TILES_DEV) % N_COL
        slot_num = slot_index % TILES_DEV
        tile_num = tile_ids[row_group, col_group, slot_num].astype(jnp.int32)
        row_block = tile_num // CB
        col_block = tile_num % CB
        alive = slot_num < tile_counts[row_group, col_group]

        def compute(state):
            row_acc, col_acc = state
            row_start = ((row_group * RB + row_block) * BLK).astype(jnp.int32)
            col_start = (col_block * BLK).astype(jnp.int32)
            zero = jnp.zeros((), jnp.int32)
            row_part = lax.dynamic_slice(row_z, (row_start, zero), (BLK, D))
            row_norm = lax.dynamic_slice(row_sq, (row_start,), (BLK,))
            row_vec = lax.dynamic_slice(row_probes, (zero, row_start), (P_SIZE, BLK))
            col_part = lax.dynamic_slice(col_z, (col_group, zero, col_start), (1, D, BLK))[0]
            col_norm = lax.dynamic_slice(col_sq, (col_group, col_start), (1, BLK))[0]
            col_vec = lax.dynamic_slice(col_probes, (col_group, zero, col_start), (1, P_SIZE, BLK))[0]
            kernel_tile = kernel_block(row_part, row_norm, col_part, col_norm, factor)
            row_part_sum = lax.dot_general(col_vec, kernel_tile, (((1,), (1,)), ((), ())), preferred_element_type=jnp.float32)
            col_part_sum = jnp.dot(row_vec, kernel_tile, preferred_element_type=jnp.float32)
            old_rows = lax.dynamic_slice(row_acc, (zero, row_start), (P_SIZE, BLK))
            row_acc = lax.dynamic_update_slice(row_acc, old_rows + row_part_sum, (zero, row_start))
            old_cols = lax.dynamic_slice(col_acc, (col_group, zero, col_start), (1, P_SIZE, BLK))
            col_acc = lax.dynamic_update_slice(col_acc, old_cols + col_part_sum[None], (col_group, zero, col_start))
            return (row_acc, col_acc)

        return lax.cond(alive, compute, lambda state: state, totals)

    row_total, col_total = lax.fori_loop(0, N_ROW * N_COL * TILES_DEV, visit_slot, (row_total, col_total))
    return row_total, col_total
```

```python
import functools
import math

import jax
import jax.numpy as jnp
from jax import lax
from jax.experimental import pallas as pl
from jax.experimental.pallas import tpu as pltpu
from jax.sharding import PartitionSpec as P

D = 128
P_SIZE = 16
N_EXTRA = 16
DEPTH = D + N_EXTRA
PACK = DEPTH + P_SIZE
HALF = PACK // 2
ROWS = 1024
COLS = 128
SLOTS = 4
N_Q = 4
N_Y = 4
N_X = 4
N_Z = 4
CHUNK = N_X * COLS
LOG2E = math.log2(math.e)
F32 = jnp.float32
BF16 = jnp.bfloat16


def split3(value):
    high = value.astype(BF16).astype(F32)
    rest = value - high
    middle = rest.astype(BF16).astype(F32)
    return high, middle, (rest - middle).astype(BF16).astype(F32)


def kernel(
    row_feats, row_probes, col_feats, col_probes, lengthscale, outputscale, tile_ids, tile_counts,
    row_out, col_out,
    row_z, row_aug, row_vec, own, chunk0, chunk1, chunk2, chunk3,
    row_part, col_part, col_sum, row_send, row_recv, s1_recv, s2_send, s2_recv, s3_send, s3_recv,
    rz_ssem, rz_rsem, z_ssem, z_rsem, g_ssem, g_rsem, rr_ssem, rr_rsem, c_ssem, c_rsem, f_ssem, f_rsem,
):
    chunks = (chunk0, chunk1, chunk2, chunk3)
    row, col = lax.axis_index("row"), lax.axis_index("col")
    y, x, z = row // (N_X * N_Z), (row // N_Z) % N_X, row % N_Z
    chip_hi, core = col // 2, col % 2
    mates = (
        chip_hi * 2 + (1 - core),
        (1 - chip_hi) * 2 + core,
        (1 - chip_hi) * 2 + (1 - core),
    )

    def in_col(yy, xx, zz):
        return ((yy * N_X + xx) * N_Z + zz, col)

    def y_peer(step):
        return (y + step) % N_Y

    def x_peer(step):
        return (x + step) % N_X

    def z_peer(step):
        return (z + step) % N_Z

    def remote(src, dst, ssem, rsem, device):
        return pltpu.make_async_remote_copy(
            src_ref=src, dst_ref=dst, send_sem=ssem, recv_sem=rsem,
            device_id=device, device_id_type=pl.DeviceIdType.MESH,
        )

    here = (row, mates[0])
    sends = []

    def send(src, dst, ssem, rsem, device):
        copy = remote(src, dst, ssem, rsem, device)
        copy.start()
        sends.append(copy)

    def received(dst, rsem):
        remote(dst, dst, rsem, rsem, here).wait_recv()

    barrier = pltpu.get_barrier_semaphore()
    greet = [(row, mate) for mate in mates]
    for step in (1, 2, 3):
        greet += [in_col(y_peer(step), x, z), in_col(y, x_peer(step), z), in_col(y, x, z_peer(step))]
    for device in greet:
        pl.semaphore_signal(barrier, inc=1, device_id=device, device_id_type=pl.DeviceIdType.MESH)

    scale = lengthscale[...]
    tall = jnp.transpose(jnp.broadcast_to(scale, (D, D)))
    col_z = (col_feats[...].astype(F32) / tall).astype(BF16)
    own[0:D] = col_z
    half_sq = -0.5 * jnp.sum(jnp.square(col_z.astype(F32)), axis=0, keepdims=True) + jnp.log(outputscale[...])
    high, middle, low = split3(half_sq)
    place = lax.broadcasted_iota(jnp.int32, (N_EXTRA, COLS), 0)
    extra = jnp.where(place < 3, 1.0, 0.0)
    for k, part in enumerate((high, middle, low)):
        extra = jnp.where(place == 3 + k, part, extra)
    own[D:DEPTH] = extra.astype(BF16)
    own[DEPTH:PACK] = col_probes[...]
    row_z[col] = (row_feats[...].astype(F32) / scale).astype(BF16)
    row_vec[col] = row_probes[...]

    pl.semaphore_wait(barrier, len(greet))

    for k in range(N_Z):
        @pl.when(z == k)
        def _():
            for step in (1, 2, 3):
                remote(own, chunks[k].at[y, x], z_ssem.at[step - 1], z_rsem.at[k], in_col(y, x, (k + step) % N_Z)).start()
            chunks[k][y, x] = own[...]
    for step in (1, 2, 3):
        sends.append(remote(own, own, z_ssem.at[step - 1], z_ssem.at[step - 1], here))
    for half in range(2):
        rows = pl.ds(half * (ROWS // 2), ROWS // 2)
        send(row_z.at[col, rows], row_z.at[col, rows], rz_ssem.at[0, half], rz_rsem.at[0, half], (row, mates[1]))
    send(row_vec.at[col], row_vec.at[col], rz_ssem.at[0, 2], rz_rsem.at[0, 2], (row, mates[1]))
    for half in range(2):
        rows = pl.ds(half * (ROWS // 2), ROWS // 2)
        send(row_z.at[col, rows], row_z.at[col, rows], rz_ssem.at[1, half], rz_rsem.at[1, half], (row, mates[0]))
    send(row_vec.at[col], row_vec.at[col], rz_ssem.at[1, 2], rz_rsem.at[1, 2], (row, mates[0]))

    def augment(q):
        zq = row_z[q]
        row_aug[q, :, 0:D] = zq
        sq = -0.5 * jnp.sum(jnp.square(zq.astype(F32)), axis=1, keepdims=True)
        high, middle, low = split3(sq)
        lane = lax.broadcasted_iota(jnp.int32, (ROWS, D), 1)
        value = jnp.where((lane >= 3) & (lane < 6), 1.0, 0.0)
        for k, part in enumerate((high, middle, low)):
            value = jnp.where(lane == k, part, value)
        row_aug[q, :, D:2 * D] = value.astype(BF16)

    def second_stage(k):
        c = chunks[k]
        for step in (1, 2, 3):
            send(c.at[y, x, 0:HALF], c.at[y, x, 0:HALF], g_ssem.at[k, 0, step - 1], g_rsem.at[k, 0, step - 1], in_col(y, x_peer(step), z))
            send(c.at[y, x, HALF:PACK], c.at[y, x, HALF:PACK], g_ssem.at[k, 1, step - 1], g_rsem.at[k, 1, step - 1], in_col(y_peer(step), x, z))

    def third_stage(k):
        c = chunks[k]
        for step in (1, 2, 3):
            received(c.at[y, x_peer(4 - step), 0:HALF], g_rsem.at[k, 0, step - 1])
        for step in (1, 2, 3):
            part = c.at[y, :, 0:HALF]
            send(part, part, g_ssem.at[k, 2, step - 1], g_rsem.at[k, 2, step - 1], in_col(y_peer(step), x, z))
        for step in (1, 2, 3):
            received(c.at[y_peer(4 - step), x, HALF:PACK], g_rsem.at[k, 1, step - 1])
        for step in (1, 2, 3):
            part = c.at[:, x, HALF:PACK]
            send(part, part, g_ssem.at[k, 3, step - 1], g_rsem.at[k, 3, step - 1], in_col(y, x_peer(step), z))

    def chunk_ready(k):
        c = chunks[k]
        for step in (1, 2, 3):
            received(c.at[y_peer(4 - step), :, 0:HALF], g_rsem.at[k, 2, step - 1])
            received(c.at[:, x_peer(4 - step), HALF:PACK], g_rsem.at[k, 3, step - 1])

    augment(col)
    for k in range(N_Z):
        @pl.when(z != k)
        def _():
            received(chunks[k].at[y, x], z_rsem.at[k])
        second_stage(k)
    third_stage(0)

    for half in range(2):
        rows = pl.ds(half * (ROWS // 2), ROWS // 2)
        received(row_z.at[mates[0], rows], rz_rsem.at[1, half])
    received(row_vec.at[mates[0]], rz_rsem.at[1, 2])
    augment(mates[0])
    for half in range(2):
        rows = pl.ds(half * (ROWS // 2), ROWS // 2)
        received(row_z.at[mates[1], rows], rz_rsem.at[0, half])
        send(row_z.at[mates[1], rows], row_z.at[mates[1], rows], rz_ssem.at[2, half], rz_rsem.at[2, half], (row, mates[0]))
    received(row_vec.at[mates[1]], rz_rsem.at[0, 2])
    send(row_vec.at[mates[1]], row_vec.at[mates[1]], rz_ssem.at[2, 2], rz_rsem.at[2, 2], (row, mates[0]))
    augment(mates[1])
    for half in range(2):
        rows = pl.ds(half * (ROWS // 2), ROWS // 2)
        received(row_z.at[mates[2], rows], rz_rsem.at[2, half])
    received(row_vec.at[mates[2]], rz_rsem.at[2, 2])
    augment(mates[2])

    count = tile_counts[0, 0]

    def compute(k):
        def visit(t, carry):
            tile = tile_ids[0, 0, t]
            i, j = (tile // 4) % 2, tile % 4
            alive = jnp.where(t < count, 1.0, 0.0).astype(F32)
            pieces = [chunks[k][j, s] for s in range(N_X)]
            right = jnp.concatenate([piece[0:DEPTH] for piece in pieces], axis=1)
            col_vec = jnp.concatenate([piece[DEPTH:PACK] for piece in pieces], axis=1)
            col_vec = (col_vec.astype(F32) * alive).astype(BF16)
            sums = jnp.zeros((P_SIZE, CHUNK), F32)
            for h in range(2):
                left = row_aug[2 * i + h, :, 0:DEPTH]
                exponent = jnp.dot(left, right, preferred_element_type=F32)
                tile_values = jnp.exp2(exponent * LOG2E).astype(BF16)
                sums += jnp.dot(row_vec[2 * i + h], tile_values, preferred_element_type=F32)
                part = lax.dot_general(
                    col_vec, tile_values, (((1,), (1,)), ((), ())), preferred_element_type=F32
                )
                row_part[t, h] = part if k == 0 else row_part[t, h] + part
            col_part[t] = sums * alive
            return carry

        lax.fori_loop(0, SLOTS, visit, 0)
        for j in range(N_Y):
            total = jnp.zeros((P_SIZE, CHUNK), F32)
            for t in range(SLOTS):
                total += jnp.where(tile_ids[0, 0, t] % 4 == j, 1.0, 0.0) * col_part[t]
            col_sum[k, j] = total

    def reduce_first(k):
        for step in (1, 2, 3):
            send(col_sum.at[k, y_peer(step)], s1_recv.at[k, step - 1], c_ssem.at[k, 0, step - 1], c_rsem.at[k, 0, step - 1], in_col(y_peer(step), x, z))

    def reduce_second(k):
        for step in (1, 2, 3):
            received(s1_recv.at[k, step - 1], c_rsem.at[k, 0, step - 1])
        total = col_sum[k, y] + s1_recv[k, 0] + s1_recv[k, 1] + s1_recv[k, 2]
        for s in range(N_X):
            s2_send[k, s] = total[:, s * COLS:(s + 1) * COLS]
        for step in (1, 2, 3):
            send(s2_send.at[k, x_peer(step)], s2_recv.at[k, step - 1], c_ssem.at[k, 1, step - 1], c_rsem.at[k, 1, step - 1], in_col(y, x_peer(step), z))

    def reduce_third(k):
        for step in (1, 2, 3):
            received(s2_recv.at[k, step - 1], c_rsem.at[k, 1, step - 1])
        s3_send[k] = s2_send[k, x] + s2_recv[k, 0] + s2_recv[k, 1] + s2_recv[k, 2]

    for k in range(N_Z):
        chunk_ready(k)
        if k + 1 < N_Z:
            third_stage(k + 1)
        if k >= 2:
            reduce_second(k - 2)
        compute(k)
        if k < N_Z - 1:
            reduce_first(k)

    for q in range(N_Q):
        total = jnp.zeros((P_SIZE, ROWS), F32)
        for t in range(SLOTS):
            total += jnp.where((tile_ids[0, 0, t] // 4) % 2 == q // 2, 1.0, 0.0) * row_part[t, q % 2]
        row_send[q] = total.astype(BF16)
    for m, mate in enumerate(mates):
        send(row_send.at[mate], row_recv.at[m], rr_ssem.at[m], rr_rsem.at[m], (row, mate))
    reduce_first(N_Z - 1)
    reduce_second(N_Z - 2)
    reduce_third(0)
    reduce_third(1)
    reduce_second(N_Z - 1)
    reduce_third(N_Z - 2)
    reduce_third(N_Z - 1)
    for step in (1, 2, 3):
        send(s3_send.at[z_peer(step)], s3_recv.at[step - 1], f_ssem.at[step - 1], f_rsem.at[step - 1], in_col(y, x, z_peer(step)))
    for m in range(3):
        received(row_recv.at[m], rr_rsem.at[m])
    row_out[...] = (
        row_send[col].astype(F32) + row_recv[0].astype(F32) + row_recv[1].astype(F32) + row_recv[2].astype(F32)
    )
    for step in (1, 2, 3):
        received(s3_recv.at[step - 1], f_rsem.at[step - 1])
    col_out[...] = s3_send[z] + s3_recv[0] + s3_recv[1] + s3_recv[2]
    for copy in sends:
        copy.wait_send()


def per_device(
    row_feats, row_probes, col_feats, col_probes, lengthscale, outputscale, tile_ids, tile_counts
):
    vmem = pl.BlockSpec(memory_space=pltpu.VMEM)
    smem = pl.BlockSpec(memory_space=pltpu.SMEM)
    dma = pltpu.SemaphoreType.DMA
    row_result, col_result = pl.pallas_call(
        kernel,
        out_shape=(
            jax.ShapeDtypeStruct((P_SIZE, ROWS), F32),
            jax.ShapeDtypeStruct((P_SIZE, COLS), F32),
        ),
        in_specs=[vmem] * 6 + [smem] * 2,
        out_specs=(vmem, vmem),
        scratch_shapes=[
            pltpu.VMEM((N_Q, ROWS, D), BF16),
            pltpu.VMEM((N_Q, ROWS, 2 * D), BF16),
            pltpu.VMEM((N_Q, P_SIZE, ROWS), BF16),
            pltpu.VMEM((PACK, COLS), BF16),
            *[pltpu.VMEM((N_Y, N_X, PACK, COLS), BF16)] * N_Z,
            pltpu.VMEM((SLOTS, 2, P_SIZE, ROWS), F32),
            pltpu.VMEM((SLOTS, P_SIZE, CHUNK), F32),
            pltpu.VMEM((N_Z, N_Y, P_SIZE, CHUNK), F32),
            pltpu.VMEM((N_Q, P_SIZE, ROWS), BF16),
            pltpu.VMEM((3, P_SIZE, ROWS), BF16),
            pltpu.VMEM((N_Z, 3, P_SIZE, CHUNK), F32),
            pltpu.VMEM((N_Z, N_X, P_SIZE, COLS), F32),
            pltpu.VMEM((N_Z, 3, P_SIZE, COLS), F32),
            pltpu.VMEM((N_Z, P_SIZE, COLS), F32),
            pltpu.VMEM((3, P_SIZE, COLS), F32),
            dma((3, 3)), dma((3, 3)),
            dma((3,)), dma((N_Z,)),
            dma((N_Z, 4, 3)), dma((N_Z, 4, 3)),
            dma((3,)), dma((3,)),
            dma((N_Z, 2, 3)), dma((N_Z, 2, 3)),
            dma((3,)), dma((3,)),
        ],
        compiler_params=pltpu.CompilerParams(
            collective_id=0, has_side_effects=True, vmem_limit_bytes=56 * 2**20
        ),
    )(
        row_feats, row_probes, col_feats[0], col_probes[0], lengthscale[None, :], outputscale[None, :],
        tile_ids, tile_counts,
    )
    return row_result, col_result[None]


def solution(mesh):
    placed = (
        P(("row", "col"), None),
        P(None, ("row", "col")),
        P("col", None, "row"),
        P("col", None, "row"),
        P(),
        P(),
        P("row", "col", None),
        P("row", "col"),
    )
    return jax.shard_map(
        per_device,
        mesh=mesh,
        in_specs=placed,
        out_specs=(P(None, ("row", "col")), P("col", None, "row")),
        check_vma=False,
    )
```

```python
import functools
import math

import jax
import jax.numpy as jnp
from jax import lax
from jax.experimental import pallas as pl
from jax.experimental.pallas import tpu as pltpu
from jax.sharding import PartitionSpec as P

D = 128
P_SIZE = 16
N_EXTRA = 16
DEPTH = D + N_EXTRA
PACK = DEPTH + P_SIZE
HALF = PACK // 2
ROWS = 1024
PARTS = (0, 512, 1024)
N_PART = len(PARTS) - 1
COLS = 128
SLOTS = 4
UNROLL = 4
N_Q = 4
N_Y = 4
N_X = 4
N_Z = 4
N_PEER = N_Y * N_X - 1
CHUNK = N_X * COLS
LOG2E = math.log2(math.e)
F32 = jnp.float32
BF16 = jnp.bfloat16


def split3(value):
    high = value.astype(BF16).astype(F32)
    rest = value - high
    middle = rest.astype(BF16).astype(F32)
    return high, middle, (rest - middle).astype(BF16).astype(F32)


def kernel(
    row_feats, row_probes, col_feats, col_probes, lengthscale_in, outputscale_in, tile_ids_in, tile_counts_in,
    row_out, col_out,
    lengthscale, outputscale, tile_ids, tile_counts, feats_in, cols_in, row_z0, row_z1, row_aug0, row_aug1, row_vec0, row_vec1, own, chunk0, chunk1, chunk2, chunk3,
    row_part0, row_part1, row_send0, row_send1, row_recv0, row_recv1, col_part, col_sum, plane_recv, z_send, z_recv,
    in_sem, rz_ssem, rz_rsem, z_ssem, z_rsem, g_ssem, g_rsem, rr_ssem, rr_rsem, c_ssem, c_rsem, f_ssem, f_rsem,
):
    chunks = (chunk0, chunk1, chunk2, chunk3)
    row_z = (row_z0, row_z1)
    row_aug = (row_aug0, row_aug1)
    row_vec = (row_vec0, row_vec1)
    row_part = (row_part0, row_part1)
    row_send = (row_send0, row_send1)
    row_recv = (row_recv0, row_recv1)
    row, col = lax.axis_index("row"), lax.axis_index("col")
    y, x, z = row // (N_X * N_Z), (row // N_Z) % N_X, row % N_Z
    chip_hi, core = col // 2, col % 2
    mates = (
        chip_hi * 2 + (1 - core),
        (1 - chip_hi) * 2 + core,
        (1 - chip_hi) * 2 + (1 - core),
    )

    def in_col(yy, xx, zz):
        return ((yy * N_X + xx) * N_Z + zz, col)

    def y_peer(step):
        return (y + step) % N_Y

    def x_peer(step):
        return (x + step) % N_X

    def z_peer(step):
        return (z + step) % N_Z

    def remote(src, dst, ssem, rsem, device):
        return pltpu.make_async_remote_copy(
            src_ref=src, dst_ref=dst, send_sem=ssem, recv_sem=rsem,
            device_id=device, device_id_type=pl.DeviceIdType.MESH,
        )

    here = (row, mates[0])
    sends = []

    def send(src, dst, ssem, rsem, device):
        copy = remote(src, dst, ssem, rsem, device)
        copy.start()
        sends.append(copy)

    def received(dst, rsem):
        remote(dst, dst, rsem, rsem, here).wait_recv()

    barrier = pltpu.get_barrier_semaphore()
    greet = [(row, mate) for mate in mates]
    greet += [in_col(y, x, z_peer(step)) for step in (1, 2, 3)]
    plane = [(step // N_X, step % N_X) for step in range(1, N_Y * N_X)]
    greet += [in_col(y_peer(dy), x_peer(dx), z) for dy, dx in plane]
    for device in greet:
        pl.semaphore_signal(barrier, inc=1, device_id=device, device_id_type=pl.DeviceIdType.MESH)

    loads = [
        pltpu.make_async_copy(lengthscale_in, lengthscale, in_sem.at[0]),
        pltpu.make_async_copy(outputscale_in, outputscale, in_sem.at[1]),
        pltpu.make_async_copy(col_feats, cols_in, in_sem.at[2]),
        pltpu.make_async_copy(col_probes, own.at[DEPTH:PACK], in_sem.at[3]),
        pltpu.make_async_copy(row_feats, feats_in, in_sem.at[4]),
        pltpu.make_async_copy(tile_ids_in, tile_ids, in_sem.at[5]),
        pltpu.make_async_copy(tile_counts_in, tile_counts, in_sem.at[6]),
    ]
    spans = [pl.ds(start, end - start) for start, end in zip(PARTS, PARTS[1:])]
    for p, span in enumerate(spans):
        loads.append(pltpu.make_async_copy(row_probes.at[:, span], row_vec[p].at[col], in_sem.at[7 + p]))
    for load in loads:
        load.start()
    for load in loads[:3]:
        load.wait()
    scale = lengthscale[...]
    tall = jnp.transpose(jnp.broadcast_to(scale, (D, D)))
    col_z = (cols_in[...].astype(F32) / tall).astype(BF16)
    own[0:D] = col_z
    gain = jnp.log(jnp.full((1, COLS), outputscale[0], F32))
    half_sq = gain - 0.5 * jnp.sum(jnp.square(col_z.astype(F32)), axis=0, keepdims=True)
    high, middle, low = split3(half_sq)
    place = lax.broadcasted_iota(jnp.int32, (N_EXTRA, COLS), 0)
    extra = jnp.where(place < 3, 1.0, 0.0)
    for k, part in enumerate((high, middle, low)):
        extra = jnp.where(place == 3 + k, part, extra)
    own[D:DEPTH] = extra.astype(BF16)
    for load in loads[3:]:
        load.wait()
    chunk0[y, x] = own[...]
    for p, span in enumerate(spans):
        row_z[p][col] = (feats_in[span].astype(F32) / scale).astype(BF16)

    pl.semaphore_wait(barrier, len(greet))

    def second_stage(s):
        c = chunks[s]
        for step in (1, 2, 3):
            send(c.at[y, x, 0:HALF], c.at[y, x, 0:HALF], g_ssem.at[s, 0, step - 1], g_rsem.at[s, 0, step - 1], in_col(y, x_peer(step), z))
            send(c.at[y, x, HALF:PACK], c.at[y, x, HALF:PACK], g_ssem.at[s, 1, step - 1], g_rsem.at[s, 1, step - 1], in_col(y_peer(step), x, z))

    def third_stage(s):
        c = chunks[s]
        for step in (1, 2, 3):
            received(c.at[y, x_peer(4 - step), 0:HALF], g_rsem.at[s, 0, step - 1])
        for step in (1, 2, 3):
            part = c.at[y, :, 0:HALF]
            send(part, part, g_ssem.at[s, 2, step - 1], g_rsem.at[s, 2, step - 1], in_col(y_peer(step), x, z))
        for step in (1, 2, 3):
            received(c.at[y_peer(4 - step), x, HALF:PACK], g_rsem.at[s, 1, step - 1])
        for step in (1, 2, 3):
            part = c.at[:, x, HALF:PACK]
            send(part, part, g_ssem.at[s, 3, step - 1], g_rsem.at[s, 3, step - 1], in_col(y, x_peer(step), z))

    def chunk_ready(s):
        c = chunks[s]
        for step in (1, 2, 3):
            received(c.at[y_peer(4 - step), :, 0:HALF], g_rsem.at[s, 2, step - 1])
            received(c.at[:, x_peer(4 - step), HALF:PACK], g_rsem.at[s, 3, step - 1])

    def send_rows(hop, q, h, mate):
        send(row_z[h].at[q], row_z[h].at[q], rz_ssem.at[hop, h, 0], rz_rsem.at[hop, h, 0], (row, mate))
        send(row_vec[h].at[q], row_vec[h].at[q], rz_ssem.at[hop, h, 1], rz_rsem.at[hop, h, 1], (row, mate))

    def rows_received(hop, q, h):
        received(row_z[h].at[q], rz_rsem.at[hop, h, 0])
        received(row_vec[h].at[q], rz_rsem.at[hop, h, 1])

    def augment(q, h):
        zq = row_z[h][q]
        row_aug[h][q, :, 0:D] = zq
        sq = -0.5 * jnp.sum(jnp.square(zq.astype(F32)), axis=1, keepdims=True)
        high, middle, low = split3(sq)
        lane = lax.broadcasted_iota(jnp.int32, zq.shape, 1)
        value = jnp.where((lane >= 3) & (lane < 6), 1.0, 0.0)
        for k, part in enumerate((high, middle, low)):
            value = jnp.where(lane == k, part, value)
        row_aug[h][q, :, D:2 * D] = value.astype(BF16)

    for step in (1, 2, 3):
        send(own, chunks[4 - step].at[y, x], z_ssem.at[step - 1], z_rsem.at[3 - step], in_col(y, x, z_peer(step)))
    second_stage(0)
    for h in range(N_PART):
        send_rows(1, col, h, mates[0])
    augment(col, 0)
    rows_received(1, mates[0], 0)
    augment(mates[0], 0)
    third_stage(0)
    for s in (1, 2, 3):
        received(chunks[s].at[y, x], z_rsem.at[s - 1])
        second_stage(s)
    send_rows(0, col, 0, mates[1])
    third_stage(1)
    third_stage(2)
    third_stage(3)
    augment(col, 1)
    rows_received(1, mates[0], 1)
    augment(mates[0], 1)
    rows_received(0, mates[1], 0)
    send_rows(2, mates[1], 0, mates[0])
    send_rows(0, col, 1, mates[1])
    augment(mates[1], 0)
    rows_received(2, mates[2], 0)
    augment(mates[2], 0)

    count = tile_counts[0, 0]
    started = set()

    def compute(s, parts):
        def visit(t, carry):
            tile = tile_ids[0, 0, t]
            i, j = (tile // 4) % 2, tile % 4
            alive = jnp.where(t < count, 1.0, 0.0).astype(F32)
            pieces = [chunks[s][j, k] for k in range(N_X)]
            right = jnp.concatenate([piece[0:DEPTH] for piece in pieces], axis=1)
            col_vec = jnp.concatenate([piece[DEPTH:PACK] for piece in pieces], axis=1)
            col_vec = (col_vec.astype(F32) * alive).astype(BF16)
            sums = jnp.zeros((P_SIZE, CHUNK), F32)
            for h in parts:
                left = row_aug[h][pl.ds(2 * i, 2)].reshape(-1, 2 * D)[:, 0:DEPTH]
                vec = jnp.concatenate([row_vec[h][2 * i], row_vec[h][2 * i + 1]], axis=1)
                exponent = jnp.dot(left, right, preferred_element_type=F32)
                tile_values = jnp.exp2(exponent * LOG2E).astype(BF16)
                sums += jnp.dot(vec, tile_values, preferred_element_type=F32)
                part = lax.dot_general(
                    col_vec, tile_values, (((1,), (1,)), ((), ())), preferred_element_type=F32
                )
                row_part[h][t] = row_part[h][t] + part if ("row", h) in started else part
            sums = sums * alive
            col_part[s, t] = col_part[s, t] + sums if ("col", s) in started else sums
            return carry

        lax.fori_loop(0, SLOTS, visit, 0, unroll=UNROLL)
        started.update([("col", s)] + [("row", h) for h in parts])

    def send_cols(s):
        for j in range(N_Y):
            total = jnp.zeros((P_SIZE, CHUNK), F32)
            for t in range(SLOTS):
                total += jnp.where(tile_ids[0, 0, t] % 4 == j, 1.0, 0.0) * col_part[s, t]
            for k in range(N_X):
                col_sum[s, j, k] = total[:, k * COLS:(k + 1) * COLS]
        for d, (dy, dx) in enumerate(plane):
            remote(col_sum.at[s, y_peer(dy), x_peer(dx)], plane_recv.at[s, d], c_ssem.at[s], c_rsem.at[s], in_col(y_peer(dy), x_peer(dx), z)).start()
        sends.append(remote(plane_recv.at[s], plane_recv.at[s], c_ssem.at[s], c_ssem.at[s], here))

    def plane_total(s):
        received(plane_recv.at[s], c_rsem.at[s])
        total = col_sum[s, y, x]
        for d in range(N_PEER):
            total += plane_recv[s, d]
        return total

    def send_plane(s):
        z_send[s - 1] = plane_total(s)
        send(z_send.at[s - 1], z_recv.at[s - 1], f_ssem.at[s - 1], f_rsem.at[s - 1], in_col(y, x, z_peer(s)))

    def send_row_sums(h):
        size = PARTS[h + 1] - PARTS[h]
        for q in range(N_Q):
            total = jnp.zeros((P_SIZE, size), F32)
            for t in range(SLOTS):
                part = row_part[h][t, :, (q % 2) * size:(q % 2 + 1) * size]
                total += jnp.where((tile_ids[0, 0, t] // 4) % 2 == q // 2, 1.0, 0.0) * part
            row_send[h][q] = total.astype(BF16)
        for m in (1, 2, 0):
            send(row_send[h].at[mates[m]], row_recv[h].at[m], rr_ssem.at[h, m], rr_rsem.at[h, m], (row, mates[m]))

    chunk_ready(0)
    compute(0, (0,))
    chunk_ready(1)
    compute(1, (0,))
    rows_received(0, mates[1], 1)
    send_rows(2, mates[1], 1, mates[0])
    augment(mates[1], 1)
    rows_received(2, mates[2], 1)
    augment(mates[2], 1)
    compute(1, (1,))
    send_cols(1)
    chunk_ready(2)
    compute(2, (0, 1,))
    send_cols(2)
    send_plane(1)
    chunk_ready(3)
    compute(3, (0, 1,))
    send_row_sums(0)
    send_cols(3)
    send_plane(2)
    compute(0, (1,))
    send_row_sums(1)
    send_cols(0)
    send_plane(3)
    col_total = plane_total(0)
    for s in (1, 2, 3):
        received(z_recv.at[s - 1], f_rsem.at[s - 1])
        col_total += z_recv[s - 1]
    col_out[...] = col_total
    for h, span in enumerate(spans):
        total = row_send[h][col].astype(F32)
        for m in range(3):
            received(row_recv[h].at[m], rr_rsem.at[h, m])
            total += row_recv[h][m].astype(F32)
        row_out[:, span] = total
    for copy in sends:
        copy.wait_send()


def per_device(
    row_feats, row_probes, col_feats, col_probes, lengthscale, outputscale, tile_ids, tile_counts
):
    vmem = pl.BlockSpec(memory_space=pltpu.VMEM)
    anywhere = pl.BlockSpec(memory_space=pl.ANY)
    dma = pltpu.SemaphoreType.DMA
    sizes = [end - start for start, end in zip(PARTS, PARTS[1:])]
    row_result, col_result = pl.pallas_call(
        kernel,
        out_shape=(
            pltpu.VMEM((P_SIZE, ROWS), F32),
            pltpu.VMEM((P_SIZE, COLS), F32),
        ),
        in_specs=[anywhere] * 8,
        out_specs=(vmem, vmem),
        scratch_shapes=[
            pltpu.VMEM((1, D), F32),
            pltpu.SMEM((1,), F32),
            pltpu.SMEM((1, 1, SLOTS), jnp.int32),
            pltpu.SMEM((1, 1), jnp.int32),
            pltpu.VMEM((ROWS, D), BF16),
            pltpu.VMEM((D, COLS), BF16),
            *[pltpu.VMEM((N_Q, size, D), BF16) for size in sizes],
            *[pltpu.VMEM((N_Q, size, 2 * D), BF16) for size in sizes],
            *[pltpu.VMEM((N_Q, P_SIZE, size), BF16) for size in sizes],
            pltpu.VMEM((PACK, COLS), BF16),
            *[pltpu.VMEM((N_Y, N_X, PACK, COLS), BF16)] * N_Z,
            *[pltpu.VMEM((SLOTS, P_SIZE, 2 * size), F32) for size in sizes],
            *[pltpu.VMEM((N_Q, P_SIZE, size), BF16) for size in sizes],
            *[pltpu.VMEM((3, P_SIZE, size), BF16) for size in sizes],
            pltpu.VMEM((N_Z, SLOTS, P_SIZE, CHUNK), F32),
            pltpu.VMEM((N_Z, N_Y, N_X, P_SIZE, COLS), F32),
            pltpu.VMEM((N_Z, N_PEER, P_SIZE, COLS), F32),
            pltpu.VMEM((3, P_SIZE, COLS), F32),
            pltpu.VMEM((3, P_SIZE, COLS), F32),
            dma((7 + N_PART,)),
            dma((3, N_PART, 2)), dma((3, N_PART, 2)),
            dma((3,)), dma((3,)),
            dma((N_Z, 4, 3)), dma((N_Z, 4, 3)),
            dma((N_PART, 3)), dma((N_PART, 3)),
            dma((N_Z,)), dma((N_Z,)),
            dma((3,)), dma((3,)),
        ],
        compiler_params=pltpu.CompilerParams(
            collective_id=0, has_side_effects=True, vmem_limit_bytes=56 * 2**20
        ),
    )(
        row_feats, row_probes, col_feats[0], col_probes[0], lengthscale[None, :], outputscale,
        tile_ids, tile_counts,
    )
    return row_result, col_result[None]


def solution(mesh):
    placed = (
        P(("row", "col"), None),
        P(None, ("row", "col")),
        P("col", None, "row"),
        P("col", None, "row"),
        P(),
        P(),
        P("row", "col", None),
        P("row", "col"),
    )
    return jax.shard_map(
        per_device,
        mesh=mesh,
        in_specs=placed,
        out_specs=(P(None, ("row", "col")), P("col", None, "row")),
        check_vma=False,
    )
```

```python
import functools
import math

import jax
import jax.numpy as jnp
from jax import lax
from jax.experimental import pallas as pl
from jax.experimental.pallas import tpu as pltpu
from jax.sharding import PartitionSpec as P

D = 128
P_SIZE = 16
N_EXTRA = 16
DEPTH = D + N_EXTRA
PACK = DEPTH + P_SIZE
HALF = PACK // 2
ROWS = 1024
PARTS = (0, 512, 1024)
N_PART = len(PARTS) - 1
COLS = 128
SLOTS = 4
UNROLL = 4
N_Q = 4
N_Y = 4
N_X = 4
N_Z = 4
N_PEER = N_Y * N_X - 1
CHUNK = N_X * COLS
LOG2E = math.log2(math.e)
F32 = jnp.float32
BF16 = jnp.bfloat16


def split3(value):
    high = value.astype(BF16).astype(F32)
    rest = value - high
    middle = rest.astype(BF16).astype(F32)
    return high, middle, (rest - middle).astype(BF16).astype(F32)


def kernel(
    row_feats, row_probes, col_feats, col_probes, lengthscale_in, outputscale_in, tile_ids_in, tile_counts_in,
    row_out, col_out,
    lengthscale, outputscale, tile_ids, tile_counts, feats_in, cols_in, row_z0, row_z1, row_aug0, row_aug1, row_vec0, row_vec1, own, chunk0, chunk1, chunk2, chunk3,
    row_part0, row_part1, row_send0, row_send1, row_recv0, row_recv1, col_part, col_sum, plane_recv, z_send, z_recv,
    in_sem, rz_ssem, rz_rsem, z_ssem, z_rsem, g_ssem, g_rsem, rr_ssem, rr_rsem, c_ssem, c_rsem, f_ssem, f_rsem,
):
    chunks = (chunk0, chunk1, chunk2, chunk3)
    row_z = (row_z0, row_z1)
    row_aug = (row_aug0, row_aug1)
    row_vec = (row_vec0, row_vec1)
    row_part = (row_part0, row_part1)
    row_send = (row_send0, row_send1)
    row_recv = (row_recv0, row_recv1)
    row, col = lax.axis_index("row"), lax.axis_index("col")
    y, x, z = row // (N_X * N_Z), (row // N_Z) % N_X, row % N_Z
    chip_hi, core = col // 2, col % 2
    mates = (
        chip_hi * 2 + (1 - core),
        (1 - chip_hi) * 2 + core,
        (1 - chip_hi) * 2 + (1 - core),
    )

    def in_col(yy, xx, zz):
        return ((yy * N_X + xx) * N_Z + zz, col)

    def y_peer(step):
        return (y + step) % N_Y

    def x_peer(step):
        return (x + step) % N_X

    def z_peer(step):
        return (z + step) % N_Z

    def remote(src, dst, ssem, rsem, device):
        return pltpu.make_async_remote_copy(
            src_ref=src, dst_ref=dst, send_sem=ssem, recv_sem=rsem,
            device_id=device, device_id_type=pl.DeviceIdType.MESH,
        )

    here = (row, mates[0])
    sends = []

    def send(src, dst, ssem, rsem, device):
        copy = remote(src, dst, ssem, rsem, device)
        copy.start()
        sends.append(copy)

    def received(dst, rsem):
        remote(dst, dst, rsem, rsem, here).wait_recv()

    barrier = pltpu.get_barrier_semaphore()
    greet = [(row, mate) for mate in mates]
    greet += [in_col(y, x, z_peer(step)) for step in (1, 2, 3)]
    plane = [(step // N_X, step % N_X) for step in range(1, N_Y * N_X)]
    greet += [in_col(y_peer(dy), x_peer(dx), z) for dy, dx in plane]
    for device in greet:
        pl.semaphore_signal(barrier, inc=1, device_id=device, device_id_type=pl.DeviceIdType.MESH)

    loads = [
        pltpu.make_async_copy(lengthscale_in, lengthscale, in_sem.at[0]),
        pltpu.make_async_copy(outputscale_in, outputscale, in_sem.at[1]),
        pltpu.make_async_copy(col_feats, cols_in, in_sem.at[2]),
        pltpu.make_async_copy(col_probes, own.at[DEPTH:PACK], in_sem.at[3]),
        pltpu.make_async_copy(row_feats, feats_in, in_sem.at[4]),
        pltpu.make_async_copy(tile_ids_in, tile_ids, in_sem.at[5]),
        pltpu.make_async_copy(tile_counts_in, tile_counts, in_sem.at[6]),
    ]
    spans = [pl.ds(start, end - start) for start, end in zip(PARTS, PARTS[1:])]
    for p, span in enumerate(spans):
        loads.append(pltpu.make_async_copy(row_probes.at[:, span], row_vec[p].at[col], in_sem.at[7 + p]))
    for load in loads:
        load.start()
    for load in loads[:3]:
        load.wait()
    scale = lengthscale[...]
    tall = jnp.transpose(jnp.broadcast_to(scale, (D, D)))
    col_z = (cols_in[...].astype(F32) / tall).astype(BF16)
    own[0:D] = col_z
    gain = jnp.log(jnp.full((1, COLS), outputscale[0], F32))
    half_sq = gain - 0.5 * jnp.sum(jnp.square(col_z.astype(F32)), axis=0, keepdims=True)
    high, middle, low = split3(half_sq)
    place = lax.broadcasted_iota(jnp.int32, (N_EXTRA, COLS), 0)
    extra = jnp.where(place < 3, 1.0, 0.0)
    for k, part in enumerate((high, middle, low)):
        extra = jnp.where(place == 3 + k, part, extra)
    own[D:DEPTH] = extra.astype(BF16)
    for load in loads[3:]:
        load.wait()
    chunk0[y, x] = own[...]
    for p, span in enumerate(spans):
        row_z[p][col] = (feats_in[span].astype(F32) / scale).astype(BF16)

    pl.semaphore_wait(barrier, len(greet))

    def second_stage(s):
        c = chunks[s]
        for step in (1, 2, 3):
            send(c.at[y, x, 0:HALF], c.at[y, x, 0:HALF], g_ssem.at[s, 0, step - 1], g_rsem.at[s, 0, step - 1], in_col(y, x_peer(step), z))
            send(c.at[y, x, HALF:PACK], c.at[y, x, HALF:PACK], g_ssem.at[s, 1, step - 1], g_rsem.at[s, 1, step - 1], in_col(y_peer(step), x, z))

    def third_stage(s):
        c = chunks[s]
        for step in (1, 2, 3):
            received(c.at[y, x_peer(4 - step), 0:HALF], g_rsem.at[s, 0, step - 1])
        for step in (1, 2, 3):
            part = c.at[y, :, 0:HALF]
            send(part, part, g_ssem.at[s, 2, step - 1], g_rsem.at[s, 2, step - 1], in_col(y_peer(step), x, z))
        for step in (1, 2, 3):
            received(c.at[y_peer(4 - step), x, HALF:PACK], g_rsem.at[s, 1, step - 1])
        for step in (1, 2, 3):
            part = c.at[:, x, HALF:PACK]
            send(part, part, g_ssem.at[s, 3, step - 1], g_rsem.at[s, 3, step - 1], in_col(y, x_peer(step), z))

    def chunk_ready(s):
        c = chunks[s]
        for step in (1, 2, 3):
            received(c.at[y_peer(4 - step), :, 0:HALF], g_rsem.at[s, 2, step - 1])
            received(c.at[:, x_peer(4 - step), HALF:PACK], g_rsem.at[s, 3, step - 1])

    def send_rows(hop, q, h, mate):
        send(row_z[h].at[q], row_z[h].at[q], rz_ssem.at[hop, h, 0], rz_rsem.at[hop, h, 0], (row, mate))
        send(row_vec[h].at[q], row_vec[h].at[q], rz_ssem.at[hop, h, 1], rz_rsem.at[hop, h, 1], (row, mate))

    def rows_received(hop, q, h):
        received(row_z[h].at[q], rz_rsem.at[hop, h, 0])
        received(row_vec[h].at[q], rz_rsem.at[hop, h, 1])

    def augment(q, h):
        zq = row_z[h][q]
        row_aug[h][q, :, 0:D] = zq
        sq = -0.5 * jnp.sum(jnp.square(zq.astype(F32)), axis=1, keepdims=True)
        high, middle, low = split3(sq)
        lane = lax.broadcasted_iota(jnp.int32, zq.shape, 1)
        value = jnp.where((lane >= 3) & (lane < 6), 1.0, 0.0)
        for k, part in enumerate((high, middle, low)):
            value = jnp.where(lane == k, part, value)
        row_aug[h][q, :, D:2 * D] = value.astype(BF16)

    for step in (1, 2, 3):
        send(own, chunks[4 - step].at[y, x], z_ssem.at[step - 1], z_rsem.at[3 - step], in_col(y, x, z_peer(step)))
    second_stage(0)
    for h in range(N_PART):
        send_rows(1, col, h, mates[0])
    augment(col, 0)
    rows_received(1, mates[0], 0)
    augment(mates[0], 0)
    third_stage(0)
    for s in (1, 2, 3):
        received(chunks[s].at[y, x], z_rsem.at[s - 1])
    send_rows(0, col, 0, mates[1])
    for s in (1, 2, 3):
        second_stage(s)
    third_stage(1)
    third_stage(2)
    third_stage(3)
    augment(col, 1)
    rows_received(1, mates[0], 1)
    augment(mates[0], 1)
    rows_received(0, mates[1], 0)
    send_rows(2, mates[1], 0, mates[0])
    send_rows(0, col, 1, mates[1])
    augment(mates[1], 0)
    rows_received(2, mates[2], 0)
    augment(mates[2], 0)

    count = tile_counts[0, 0]
    started = set()

    def compute(s, parts):
        def visit(t, carry):
            tile = tile_ids[0, 0, t]
            i, j = (tile // 4) % 2, tile % 4
            alive = jnp.where(t < count, 1.0, 0.0).astype(F32)
            pieces = [chunks[s][j, k] for k in range(N_X)]
            right = jnp.concatenate([piece[0:DEPTH] for piece in pieces], axis=1)
            col_vec = jnp.concatenate([piece[DEPTH:PACK] for piece in pieces], axis=1)
            col_vec = (col_vec.astype(F32) * alive).astype(BF16)
            sums = jnp.zeros((P_SIZE, CHUNK), F32)
            for h in parts:
                left = row_aug[h][pl.ds(2 * i, 2)].reshape(-1, 2 * D)[:, 0:DEPTH]
                vec = jnp.concatenate([row_vec[h][2 * i], row_vec[h][2 * i + 1]], axis=1)
                exponent = jnp.dot(left, right, preferred_element_type=F32)
                tile_values = jnp.exp2(exponent * LOG2E).astype(BF16)
                sums += jnp.dot(vec, tile_values, preferred_element_type=F32)
                part = lax.dot_general(
                    col_vec, tile_values, (((1,), (1,)), ((), ())), preferred_element_type=F32
                )
                row_part[h][t] = row_part[h][t] + part if ("row", h) in started else part
            sums = sums * alive
            col_part[s, t] = col_part[s, t] + sums if ("col", s) in started else sums
            return carry

        lax.fori_loop(0, SLOTS, visit, 0, unroll=UNROLL)
        started.update([("col", s)] + [("row", h) for h in parts])

    def send_cols(s):
        for j in range(N_Y):
            total = jnp.zeros((P_SIZE, CHUNK), F32)
            for t in range(SLOTS):
                total += jnp.where(tile_ids[0, 0, t] % 4 == j, 1.0, 0.0) * col_part[s, t]
            for k in range(N_X):
                col_sum[s, j, k] = total[:, k * COLS:(k + 1) * COLS].astype(BF16)
        for d, (dy, dx) in enumerate(plane):
            remote(col_sum.at[s, y_peer(dy), x_peer(dx)], plane_recv.at[s, d], c_ssem.at[s], c_rsem.at[s], in_col(y_peer(dy), x_peer(dx), z)).start()
        sends.append(remote(plane_recv.at[s], plane_recv.at[s], c_ssem.at[s], c_ssem.at[s], here))

    def plane_total(s):
        received(plane_recv.at[s], c_rsem.at[s])
        total = col_sum[s, y, x].astype(F32)
        for d in range(N_PEER):
            total += plane_recv[s, d].astype(F32)
        return total

    def send_plane(s):
        z_send[s - 1] = plane_total(s)
        send(z_send.at[s - 1], z_recv.at[s - 1], f_ssem.at[s - 1], f_rsem.at[s - 1], in_col(y, x, z_peer(s)))

    def send_row_sums(h):
        size = PARTS[h + 1] - PARTS[h]
        for q in range(N_Q):
            total = jnp.zeros((P_SIZE, size), F32)
            for t in range(SLOTS):
                part = row_part[h][t, :, (q % 2) * size:(q % 2 + 1) * size]
                total += jnp.where((tile_ids[0, 0, t] // 4) % 2 == q // 2, 1.0, 0.0) * part
            row_send[h][q] = total.astype(BF16)
        for m in (1, 2, 0):
            send(row_send[h].at[mates[m]], row_recv[h].at[m], rr_ssem.at[h, m], rr_rsem.at[h, m], (row, mates[m]))

    chunk_ready(0)
    compute(0, (0,))
    chunk_ready(1)
    compute(1, (0,))
    rows_received(0, mates[1], 1)
    send_rows(2, mates[1], 1, mates[0])
    augment(mates[1], 1)
    rows_received(2, mates[2], 1)
    augment(mates[2], 1)
    compute(1, (1,))
    send_cols(1)
    chunk_ready(2)
    compute(2, (0, 1,))
    send_cols(2)
    send_plane(1)
    chunk_ready(3)
    compute(3, (0, 1,))
    send_row_sums(0)
    send_cols(3)
    send_plane(2)
    compute(0, (1,))
    send_row_sums(1)
    send_cols(0)
    send_plane(3)
    col_total = plane_total(0)
    for s in (1, 2, 3):
        received(z_recv.at[s - 1], f_rsem.at[s - 1])
        col_total += z_recv[s - 1]
    col_out[...] = col_total
    for h, span in enumerate(spans):
        total = row_send[h][col].astype(F32)
        for m in range(3):
            received(row_recv[h].at[m], rr_rsem.at[h, m])
            total += row_recv[h][m].astype(F32)
        row_out[:, span] = total
    for copy in sends:
        copy.wait_send()


def per_device(
    row_feats, row_probes, col_feats, col_probes, lengthscale, outputscale, tile_ids, tile_counts
):
    vmem = pl.BlockSpec(memory_space=pltpu.VMEM)
    anywhere = pl.BlockSpec(memory_space=pl.ANY)
    dma = pltpu.SemaphoreType.DMA
    sizes = [end - start for start, end in zip(PARTS, PARTS[1:])]
    row_result, col_result = pl.pallas_call(
        kernel,
        out_shape=(
            pltpu.VMEM((P_SIZE, ROWS), F32),
            pltpu.VMEM((P_SIZE, COLS), F32),
        ),
        in_specs=[anywhere] * 8,
        out_specs=(vmem, vmem),
        scratch_shapes=[
            pltpu.VMEM((1, D), F32),
            pltpu.SMEM((1,), F32),
            pltpu.SMEM((1, 1, SLOTS), jnp.int32),
            pltpu.SMEM((1, 1), jnp.int32),
            pltpu.VMEM((ROWS, D), BF16),
            pltpu.VMEM((D, COLS), BF16),
            *[pltpu.VMEM((N_Q, size, D), BF16) for size in sizes],
            *[pltpu.VMEM((N_Q, size, 2 * D), BF16) for size in sizes],
            *[pltpu.VMEM((N_Q, P_SIZE, size), BF16) for size in sizes],
            pltpu.VMEM((PACK, COLS), BF16),
            *[pltpu.VMEM((N_Y, N_X, PACK, COLS), BF16)] * N_Z,
            *[pltpu.VMEM((SLOTS, P_SIZE, 2 * size), F32) for size in sizes],
            *[pltpu.VMEM((N_Q, P_SIZE, size), BF16) for size in sizes],
            *[pltpu.VMEM((3, P_SIZE, size), BF16) for size in sizes],
            pltpu.VMEM((N_Z, SLOTS, P_SIZE, CHUNK), F32),
            pltpu.VMEM((N_Z, N_Y, N_X, P_SIZE, COLS), BF16),
            pltpu.VMEM((N_Z, N_PEER, P_SIZE, COLS), BF16),
            pltpu.VMEM((3, P_SIZE, COLS), F32),
            pltpu.VMEM((3, P_SIZE, COLS), F32),
            dma((7 + N_PART,)),
            dma((3, N_PART, 2)), dma((3, N_PART, 2)),
            dma((3,)), dma((3,)),
            dma((N_Z, 4, 3)), dma((N_Z, 4, 3)),
            dma((N_PART, 3)), dma((N_PART, 3)),
            dma((N_Z,)), dma((N_Z,)),
            dma((3,)), dma((3,)),
        ],
        compiler_params=pltpu.CompilerParams(
            collective_id=0, has_side_effects=True, vmem_limit_bytes=56 * 2**20
        ),
    )(
        row_feats, row_probes, col_feats[0], col_probes[0], lengthscale[None, :], outputscale,
        tile_ids, tile_counts,
    )
    return row_result, col_result[None]


def solution(mesh):
    placed = (
        P(("row", "col"), None),
        P(None, ("row", "col")),
        P("col", None, "row"),
        P("col", None, "row"),
        P(),
        P(),
        P("row", "col", None),
        P("row", "col"),
    )
    return jax.shard_map(
        per_device,
        mesh=mesh,
        in_specs=placed,
        out_specs=(P(None, ("row", "col")), P("col", None, "row")),
        check_vma=False,
    )
```
